32 devices in a mesh: gx: 2 (over x), gy: 16 (over z, y, core).
Axes of the slice: x: 2, y: 2, z: 4, core: 2. Of those that a mesh axis runs over, the one named last changes fastest.
Arguments:
- vectors: bfloat16 [8192, 32, 128], P(('gx', 'gy')), may hold values from -6 to 6
- coupling_table: bfloat16 [5, 16, 128, 128], replicated, may hold values from -0.375 to 0.375
- factor_index: int32 [8192, 5, 2], P(('gx', 'gy')), may hold values from 0 to 15
- level_order: int32 [5], replicated, may hold values from 0 to 4, each once
Outputs:
- applied: bfloat16 [8192, 32, 128], P(('gx', 'gy'))
The draws below stay inside these ranges and needn't reach their ends.
Inputs may be any that keep to these rules, and one draw needn't show every extreme that they name: `factor_index`: table entries of the coupling matrices. `level_order`: each level slot appears once.
All inputs are finite; a program needn't handle non-finite values.
Results may differ from the reference program's by a relative error of at most 0.0086.
Values may be sent and summed in bfloat16 or wider, within the bound.
No kernel may reach another device: no remote copies, remote signals or barrier semaphores. Data moves between devices by JAX's collectives and lax.ppermute only.
A program may use at most 64 MiB of HBM per device.

```python
import jax
import jax.numpy as jnp
from jax import lax

R = 128
NRHS = 32
NTAB = 16
BLK_DEV = 256
BLOCKS = 8192
LEVELS = 5


def place_ends(array, own_key, smallest, largest):
    longest = array.shape.index(max(array.shape))
    spots = []
    for shift in (0, 1):
        where = [jax.random.randint(jax.random.fold_in(own_key, axis), (), 0, length) for axis, length in enumerate(array.shape)]
        where[longest] = (where[longest] + shift) % array.shape[longest]
        spots.append(tuple(where))
    return array.at[spots[0]].set(smallest).at[spots[1]].set(largest)


def shard_levels(own_key, extent, shards, low, top_value):
    gain = 1.0
    for dim, shards_of in shards:
        draws = jax.random.uniform(jax.random.fold_in(jax.random.fold_in(own_key, 6), dim), (shards_of,), jnp.float32, low / len(shards), top_value / len(shards))
        gain = gain * jnp.repeat(jnp.exp(draws), extent[dim] // shards_of).reshape((-1,) + (1,) * (len(extent) - 1 - dim))
    return gain


def normal_values(key, shape, width, reach, pieces=(), held_as=jnp.bfloat16):
    factor_of = shard_levels(key, shape, pieces, -0.22, 0.18) if pieces else 1.0
    drawn = jax.random.normal(key, shape, jnp.float32) * width * factor_of
    return jnp.minimum(jnp.maximum(drawn, -reach), reach).astype(held_as)


def setup_inputs(seed: int = 0) -> dict:
    keys = jax.random.split(jax.random.key(seed), 5)
    return {
        "vectors": normal_values(keys[0], (BLOCKS, NRHS, R), 1.0, 6.0, ((0, 32),)),
        "coupling_table": normal_values(keys[1], (LEVELS, NTAB, R, R), (2 * R) ** -0.5, 0.375),
        "factor_index": place_ends(jax.random.randint(keys[2], (BLOCKS, LEVELS, 2), 0, NTAB), jax.random.fold_in(keys[2], 1), 0, NTAB - 1).astype(jnp.int32),
        "level_order": jax.random.permutation(keys[3], LEVELS).astype(jnp.int32),
    }


def reference(vectors, coupling_table, factor_index, level_order):
    field = vectors
    block_ids = jnp.arange(BLOCKS, dtype=jnp.int32)
    groups = BLOCKS // BLK_DEV
    for position in range(LEVELS):
        level_slot = level_order[position]
        level_table = lax.dynamic_index_in_dim(coupling_table, level_slot, 0, keepdims=False).astype(jnp.float32)
        chosen = lax.dynamic_index_in_dim(factor_index, level_slot, 1, keepdims=False)
        partner = jnp.take(field, block_ids ^ (BLK_DEV << position), axis=0)

        def one_group(operands):
            own_blocks, other_blocks, selected = operands
            first = level_table[selected[:, 0]]
            second = level_table[selected[:, 1]]
            local_part = jnp.einsum("bnj,bij->bni", own_blocks.astype(jnp.float32), first)
            remote_part = jnp.einsum("bnj,bij->bni", other_blocks.astype(jnp.float32), second)
            return (local_part + remote_part).astype(jnp.bfloat16)

        field = lax.map(one_group, (field.reshape(groups, BLK_DEV, NRHS, R),
                                    partner.reshape(groups, BLK_DEV, NRHS, R),
                                    chosen.reshape(groups, BLK_DEV, 2))).reshape(BLOCKS, NRHS, R)
    return field
```

```python
import functools
import math

import jax
import jax.numpy as jnp
from jax import lax
from jax.experimental import pallas as pl
from jax.experimental.pallas import tpu as pltpu
from jax.sharding import PartitionSpec as P

AXES = ("gx", "gy")
LOAD_FACTOR = 7
PACK_PARAMS = pltpu.CompilerParams(vmem_limit_bytes=58 * 1024 * 1024)
PARAMS = pltpu.CompilerParams(vmem_limit_bytes=24 * 1024 * 1024)


def all_levels_kernel(offset, rhs, order_ref, index_ref, field_ref, table_ref, out_ref, even, odd, in_sems, out_sem):
    devices, rows, rank = out_ref.shape
    share = rows // rhs
    levels = order_ref.shape[0]
    pairs = devices // 2
    group = min(pairs, 1 << (48 // share).bit_length() - 1)
    part = min(group, 8)

    def arrival(p):
        some = pl.ds(p * 2 * part, 2 * part)
        return pltpu.make_async_copy(
            field_ref.at[some, pl.ds(rhs * offset, rows)], even.at[some], in_sems.at[p]
        )

    for p in range(pairs // part):
        arrival(p).start()

    for level in range(levels):
        source, target = ((even, odd), (odd, even))[level % 2]
        slot = order_ref[level]

        def entries(d, j):
            at = ((offset + j) * levels + slot) * 2
            return table_ref[slot, index_ref[d, at]], table_ref[slot, index_ref[d, at + 1]]

        def one_group(step, carry):
            for k in range(group):
                if level == 0 and k % part == 0:
                    arrival(step * (group // part) + k // part).wait()
                pair = step * group + k
                low = ((pair >> level) << (level + 1)) | (pair & ((1 << level) - 1))
                high = low + (1 << level)
                for j in range(share):
                    block = pl.ds(rhs * j, rhs)
                    both = jnp.concatenate([source[low, block], source[high, block]], axis=1)
                    low_own, low_other = entries(low, j)
                    high_own, high_other = entries(high, j)
                    coupling = jnp.concatenate(
                        [jnp.concatenate([low_own, low_other], axis=0), jnp.concatenate([high_other, high_own], axis=0)],
                        axis=1,
                    )
                    product = jnp.dot(both, coupling, preferred_element_type=jnp.float32).astype(jnp.bfloat16)
                    target[low, block] = product[:, :rank]
                    target[high, block] = product[:, rank:]
                if level == levels - 1 and k % part == part - 1:
                    for first in (pair - part + 1, pairs + pair - part + 1):
                        done = pl.ds(first, part)
                        pltpu.make_async_copy(target.at[done], out_ref.at[done], out_sem).start()
            return carry

        lax.fori_loop(0, pairs // group, one_group, 0)
    last = (even, odd)[levels % 2]
    pltpu.make_async_copy(last, out_ref, out_sem).wait()


def apply_all_levels(payload, offset, share, rhs, table, index, order):
    devices, _, rank = payload.shape
    levels = table.shape[0]
    shape = (devices, share * rhs, rank)
    blocks = devices * share
    return pl.pallas_call(
        functools.partial(all_levels_kernel, offset, rhs),
        grid_spec=pltpu.PrefetchScalarGridSpec(
            num_scalar_prefetch=2,
            grid=(),
            in_specs=[pl.BlockSpec(memory_space=pltpu.HBM), pl.BlockSpec(memory_space=pltpu.VMEM)],
            out_specs=pl.BlockSpec(memory_space=pltpu.HBM),
            scratch_shapes=[pltpu.VMEM(shape, jnp.bfloat16)] * 2
            + [pltpu.SemaphoreType.DMA((devices // 2,)), pltpu.SemaphoreType.DMA],
        ),
        out_shape=jax.ShapeDtypeStruct(shape, jnp.bfloat16),
        compiler_params=PARAMS,
        cost_estimate=pl.CostEstimate(
            flops=LOAD_FACTOR * levels * blocks * 4 * rhs * rank * rank,
            bytes_accessed=2 * (2 * blocks * rhs * rank + table.size),
            transcendentals=0,
        ),
    )(order, index, payload, table)


def pack_kernel(units, vectors_ref, index_ref, out_ref, held, in_sems, out_sems):
    devices, rows, rank = out_ref.shape
    rhs = vectors_ref.shape[1]
    levels, _, blocks = index_ref.shape
    used = units * rhs
    parts = in_sems.shape[0]
    size = devices // parts
    source = vectors_ref.at[pl.ds(0, devices * units)].reshape(devices, used, rank)
    inward = [
        pltpu.make_async_copy(
            source.at[pl.ds(p * size, size)], held.at[pl.ds(p * size, size), pl.ds(0, used)], in_sems.at[p]
        )
        for p in range(parts)
    ]
    for copy in inward:
        copy.start()

    def pick(shape, condition):
        first, second = (lax.broadcasted_iota(jnp.int32, shape, dim) for dim in (0, 1))
        return condition(first, second).astype(jnp.float32).astype(jnp.bfloat16)

    def product(left, right, contract):
        return lax.dot_general(left, right, ((contract[:1], contract[1:]), ((), ())), preferred_element_type=jnp.float32)

    width = -(-2 * levels // 16) * 16
    entries = jnp.zeros((width, blocks), jnp.float32)
    for slot in range(levels):
        spot = pick((width, 2), lambda r, t: r == 2 * slot + t)
        entries += product(spot, index_ref[slot].astype(jnp.float32).astype(jnp.bfloat16), (1, 0))
    entries = entries.astype(jnp.bfloat16)
    lanes = jnp.zeros((devices, rank), jnp.float32)
    for unit in range(units):
        chosen = product(pick((devices, blocks), lambda d, b: b == d * units + unit), entries, (1, 1))
        spot = pick((width, rank), lambda r, lane: (lane == unit * 2 * levels + r) & (r < 2 * levels))
        lanes += product(chosen.astype(jnp.bfloat16), spot, (1, 0))
    for d in range(devices):
        held[d, pl.ds(used, rows - used)] = jnp.broadcast_to(lanes[d : d + 1], (rows - used, rank)).astype(jnp.bfloat16)

    outward = [
        pltpu.make_async_copy(held.at[pl.ds(p * size, size)], out_ref.at[pl.ds(p * size, size)], out_sems.at[p])
        for p in range(parts)
    ]
    for arrival, departure in zip(inward, outward):
        arrival.wait()
        departure.start()
    for copy in outward:
        copy.wait()


def pack(vectors, factor_index, devices, units):
    blocks, rhs, rank = vectors.shape
    levels = factor_index.shape[1]
    assert units * levels * 2 <= rank
    shape = (devices, units * rhs + 8, rank)
    parts = 8
    return pl.pallas_call(
        functools.partial(pack_kernel, units),
        in_specs=[pl.BlockSpec(memory_space=pltpu.HBM), pl.BlockSpec(memory_space=pltpu.VMEM)],
        out_specs=pl.BlockSpec(memory_space=pltpu.HBM),
        out_shape=jax.ShapeDtypeStruct(shape, jnp.bfloat16),
        scratch_shapes=[pltpu.VMEM(shape, jnp.bfloat16)] + [pltpu.SemaphoreType.DMA((parts,))] * 2,
        compiler_params=PACK_PARAMS,
        cost_estimate=pl.CostEstimate(flops=0, bytes_accessed=4 * vectors.size, transcendentals=0),
    )(vectors, jnp.transpose(factor_index, (1, 2, 0)))


def one_level_kernel(level, order_ref, index_ref, own_ref, other_ref, table_ref, out_ref):
    levels = order_ref.shape[0]
    slot = order_ref[level]

    def one_block(b, carry):
        at = (b * levels + slot) * 2
        both = jnp.concatenate([own_ref[b], other_ref[b]], axis=1)
        coupling = jnp.concatenate([table_ref[slot, index_ref[at]], table_ref[slot, index_ref[at + 1]]], axis=0)
        out_ref[b] = jnp.dot(both, coupling, preferred_element_type=jnp.float32).astype(jnp.bfloat16)
        return carry

    lax.fori_loop(0, own_ref.shape[0], one_block, 0, unroll=16)


def apply_level(own, other, table, index, order, level):
    blocks, rhs, rank = own.shape
    return pl.pallas_call(
        functools.partial(one_level_kernel, level),
        grid_spec=pltpu.PrefetchScalarGridSpec(
            num_scalar_prefetch=2,
            grid=(),
            in_specs=[pl.BlockSpec(memory_space=pltpu.VMEM)] * 3,
            out_specs=pl.BlockSpec(memory_space=pltpu.VMEM),
        ),
        out_shape=jax.ShapeDtypeStruct(own.shape, jnp.bfloat16),
        compiler_params=PARAMS,
        cost_estimate=pl.CostEstimate(
            flops=LOAD_FACTOR * blocks * 4 * rhs * rank * rank,
            bytes_accessed=2 * (3 * own.size + table.size),
            transcendentals=0,
        ),
    )(order, index, own, other, table)


def place_kernel(shares, starts, aliased, *refs):
    count = len(shares)
    pieces = refs[aliased : aliased + count]
    out_ref = refs[aliased + count]
    held = refs[aliased + count + 1 : aliased + 2 * count + 1]
    in_sems, out_sems = refs[aliased + 2 * count + 1 :]
    moves = []
    for c, (piece, share, (first, units)) in enumerate(zip(pieces, shares, starts)):
        groups = piece.shape[0]
        target = out_ref.at[pl.ds(first[0], groups * units)].reshape((groups, units) + out_ref.shape[1:])
        parts = 4 if groups % 4 == 0 else 1
        for p in range(parts):
            some = pl.ds(p * (groups // parts), groups // parts)
            at = len(moves)
            moves.append((
                pltpu.make_async_copy(piece.at[some], held[c].at[some], in_sems.at[at]),
                pltpu.make_async_copy(
                    held[c].at[some], target.at[some, pl.ds(first[1], share)], out_sems.at[at]
                ),
            ))
    for inward, _ in moves:
        inward.start()
    for inward, outward in moves:
        inward.wait()
        outward.start()
    for _, outward in moves:
        outward.wait()


def place(result, shape, pieces, starts):
    aliased = int(result is not None)
    operands = ([result] if aliased else []) + pieces
    return pl.pallas_call(
        functools.partial(place_kernel, [p.shape[1] for p in pieces], starts, aliased),
        in_specs=[pl.BlockSpec(memory_space=pltpu.HBM)] * len(operands),
        out_specs=pl.BlockSpec(memory_space=pltpu.HBM),
        out_shape=jax.ShapeDtypeStruct(shape, jnp.bfloat16),
        scratch_shapes=[pltpu.VMEM(p.shape, jnp.bfloat16) for p in pieces]
        + [pltpu.SemaphoreType.DMA((4 * len(pieces),))] * 2,
        input_output_aliases={0: 0} if aliased else {},
        compiler_params=PARAMS,
        cost_estimate=pl.CostEstimate(
            flops=0, bytes_accessed=4 * sum(p.size for p in pieces), transcendentals=0
        ),
    )(*operands)


def body(vectors, coupling_table, factor_index, level_order):
    devices = lax.axis_size("gx") * lax.axis_size("gy")
    middle_bits = lax.axis_size("gy").bit_length() - 1
    levels = coupling_table.shape[0]
    blocks, rhs, rank = vectors.shape
    units = blocks // devices
    far_units = units - units // 8
    first = (far_units + 1) // 4
    shares = [first, far_units - first] if first else [far_units]
    starts = [sum(shares[:c]) for c in range(len(shares) + 1)]
    spread = devices * far_units

    def exchange(array):
        return lax.all_to_all(array, AXES, split_axis=0, concat_axis=0, tiled=True)

    def partner(array, level):
        axis, bit = ("gy", level) if level < middle_bits else ("gx", level - middle_bits)
        return lax.ppermute(array, axis, [(i, i ^ 1 << bit) for i in range(lax.axis_size(axis))])

    def near_level(near, level):
        return apply_level(near, partner(near, level), table, near_index, level_order, level)

    arrived = exchange(pack(vectors, factor_index, devices, far_units))
    table = jnp.swapaxes(coupling_table, 2, 3)

    near = vectors[spread:]
    near_index = factor_index[spread:].reshape(-1)
    if units > far_units:
        for level in range(middle_bits - 1):
            near = near_level(near, level)
        arrived, near = lax.optimization_barrier((arrived, near))
    index = arrived[:, far_units * rhs].astype(jnp.int32)

    done = []
    other = None
    for c, share in enumerate(shares):
        if c == 1:
            other = partner(near, middle_bits - 1)
            arrived, other = lax.optimization_barrier((arrived, other))
        far = apply_all_levels(arrived, starts[c], share, rhs, table, index, level_order)
        done.append(exchange(far).reshape(devices, share, rhs, rank))
    if units == far_units:
        return jnp.concatenate(done, axis=1).reshape(vectors.shape)
    if other is None:
        other = partner(near, middle_bits - 1)
    near = apply_level(near, other, table, near_index, level_order, middle_bits - 1)
    for level in range(middle_bits, levels):
        near = near_level(near, level)
    at = [((0, start), far_units) for start in starts]
    near_at = ((spread, 0), blocks - spread)
    result = place(None, vectors.shape, done[:-1] + [near[None]], at[: len(done) - 1] + [near_at])
    return place(result, vectors.shape, done[-1:], at[len(done) - 1 : len(done)])


def solution(mesh):
    placed = (P(AXES, None, None), P(), P(AXES, None, None), P())
    return jax.shard_map(
        body, mesh=mesh, in_specs=placed, out_specs=P(AXES, None, None), check_vma=False
    )
```

```python
import functools
import math

import jax
import jax.numpy as jnp
from jax import lax
from jax.experimental import pallas as pl
from jax.experimental.pallas import tpu as pltpu
from jax.sharding import PartitionSpec as P

AXES = ("gx", "gy")
LOAD_FACTOR = 7
HEAVY = 50
PACK_PARAMS = pltpu.CompilerParams(vmem_limit_bytes=58 * 1024 * 1024)
PARAMS = pltpu.CompilerParams(vmem_limit_bytes=24 * 1024 * 1024)


def all_levels_kernel(order_ref, index_ref, field_ref, table_ref, out_ref, even, odd):
    devices, share, rhs, rank = out_ref.shape
    levels = order_ref.shape[0]
    for level in range(levels):
        target = out_ref if level == levels - 1 else (even, odd)[(level + 1) % 2]
        slot = order_ref[level]

        def load(d, j):
            if level == 0:
                return field_ref[d, pl.ds(rhs * j, rhs), :]
            return (even, odd)[level % 2][d, j]

        def entries(d, j):
            at = (j * levels + slot) * 2
            return table_ref[slot, index_ref[d, at]], table_ref[slot, index_ref[d, at + 1]]

        def one_pair(pair, carry):
            low = ((pair >> level) << (level + 1)) | (pair & ((1 << level) - 1))
            high = low + (1 << level)
            for j in range(share):
                both = jnp.concatenate([load(low, j), load(high, j)], axis=1)
                low_own, low_other = entries(low, j)
                high_own, high_other = entries(high, j)
                coupling = jnp.concatenate(
                    [jnp.concatenate([low_own, low_other], axis=0), jnp.concatenate([high_other, high_own], axis=0)],
                    axis=1,
                )
                product = jnp.dot(both, coupling, preferred_element_type=jnp.float32).astype(jnp.bfloat16)
                target[low, j] = product[:, :rank]
                target[high, j] = product[:, rank:]
            return carry

        lax.fori_loop(0, devices // 2, one_pair, 0, unroll=8)


def apply_all_levels(payload, share, rhs, table, index, order):
    devices, _, rank = payload.shape
    levels = table.shape[0]
    shape = (devices, share, rhs, rank)
    blocks = devices * share
    return pl.pallas_call(
        all_levels_kernel,
        grid_spec=pltpu.PrefetchScalarGridSpec(
            num_scalar_prefetch=2,
            grid=(),
            in_specs=[pl.BlockSpec(memory_space=pltpu.VMEM)] * 2,
            out_specs=pl.BlockSpec(memory_space=pltpu.VMEM),
            scratch_shapes=[pltpu.VMEM(shape, jnp.bfloat16)] * 2,
        ),
        out_shape=jax.ShapeDtypeStruct(shape, jnp.bfloat16),
        compiler_params=PARAMS,
        cost_estimate=pl.CostEstimate(
            flops=levels * blocks * 4 * rhs * rank * rank,
            bytes_accessed=2 * (2 * blocks * rhs * rank + table.size),
            transcendentals=0,
        ),
    )(order, index, payload, table)


def pack_kernel(units, vectors_ref, index_ref, out_ref, held, in_sems, out_sems):
    devices, rows, rank = out_ref.shape
    rhs = vectors_ref.shape[1]
    levels, _, blocks = index_ref.shape
    used = units * rhs
    parts = in_sems.shape[0]
    size = devices // parts
    source = vectors_ref.at[pl.ds(0, devices * units)].reshape(devices, used, rank)
    inward = [
        pltpu.make_async_copy(
            source.at[pl.ds(p * size, size)], held.at[pl.ds(p * size, size), pl.ds(0, used)], in_sems.at[p]
        )
        for p in range(parts)
    ]
    for copy in inward:
        copy.start()

    def pick(shape, condition):
        first, second = (lax.broadcasted_iota(jnp.int32, shape, dim) for dim in (0, 1))
        return condition(first, second).astype(jnp.float32).astype(jnp.bfloat16)

    def product(left, right, contract):
        return lax.dot_general(left, right, ((contract[:1], contract[1:]), ((), ())), preferred_element_type=jnp.float32)

    width = -(-2 * levels // 16) * 16
    entries = jnp.zeros((width, blocks), jnp.float32)
    for slot in range(levels):
        spot = pick((width, 2), lambda r, t: r == 2 * slot + t)
        entries += product(spot, index_ref[slot].astype(jnp.float32).astype(jnp.bfloat16), (1, 0))
    entries = entries.astype(jnp.bfloat16)
    lanes = jnp.zeros((devices, rank), jnp.float32)
    for unit in range(units):
        chosen = product(pick((devices, blocks), lambda d, b: b == d * units + unit), entries, (1, 1))
        spot = pick((width, rank), lambda r, lane: (lane == unit * 2 * levels + r) & (r < 2 * levels))
        lanes += product(chosen.astype(jnp.bfloat16), spot, (1, 0))
    for d in range(devices):
        held[d, pl.ds(used, rows - used)] = jnp.broadcast_to(lanes[d : d + 1], (rows - used, rank)).astype(jnp.bfloat16)

    outward = [
        pltpu.make_async_copy(held.at[pl.ds(p * size, size)], out_ref.at[pl.ds(p * size, size)], out_sems.at[p])
        for p in range(parts)
    ]
    for arrival, departure in zip(inward, outward):
        arrival.wait()
        departure.start()
    for copy in outward:
        copy.wait()


def pack(vectors, factor_index, devices, units):
    blocks, rhs, rank = vectors.shape
    levels = factor_index.shape[1]
    assert units * levels * 2 <= rank
    shape = (devices, units * rhs + 8, rank)
    parts = 8
    return pl.pallas_call(
        functools.partial(pack_kernel, units),
        in_specs=[pl.BlockSpec(memory_space=pltpu.HBM), pl.BlockSpec(memory_space=pltpu.VMEM)],
        out_specs=pl.BlockSpec(memory_space=pltpu.HBM),
        out_shape=jax.ShapeDtypeStruct(shape, jnp.bfloat16),
        scratch_shapes=[pltpu.VMEM(shape, jnp.bfloat16)] + [pltpu.SemaphoreType.DMA((parts,))] * 2,
        compiler_params=PACK_PARAMS,
        cost_estimate=pl.CostEstimate(flops=0, bytes_accessed=4 * vectors.size, transcendentals=0),
    )(vectors, jnp.transpose(factor_index, (1, 2, 0)))


def one_level_kernel(level, offset, order_ref, index_ref, own_ref, other_ref, table_ref, out_ref):
    levels = order_ref.shape[0]
    slot = order_ref[level]

    def one_block(b, carry):
        at = ((offset + b) * levels + slot) * 2
        both = jnp.concatenate([own_ref[b], other_ref[b]], axis=1)
        coupling = jnp.concatenate([table_ref[slot, index_ref[at]], table_ref[slot, index_ref[at + 1]]], axis=0)
        out_ref[b] = jnp.dot(both, coupling, preferred_element_type=jnp.float32).astype(jnp.bfloat16)
        return carry

    lax.fori_loop(0, own_ref.shape[0], one_block, 0, unroll=16)


def apply_level(own, other, table, index, order, level, offset=0, weight=1):
    blocks, rhs, rank = own.shape
    return pl.pallas_call(
        functools.partial(one_level_kernel, level, offset),
        grid_spec=pltpu.PrefetchScalarGridSpec(
            num_scalar_prefetch=2,
            grid=(),
            in_specs=[pl.BlockSpec(memory_space=pltpu.VMEM)] * 3,
            out_specs=pl.BlockSpec(memory_space=pltpu.VMEM),
        ),
        out_shape=jax.ShapeDtypeStruct(own.shape, jnp.bfloat16),
        compiler_params=PARAMS,
        cost_estimate=pl.CostEstimate(
            flops=weight * LOAD_FACTOR * blocks * 4 * rhs * rank * rank,
            bytes_accessed=2 * (3 * own.size + table.size),
            transcendentals=0,
        ),
    )(order, index, own, other, table)


def place_kernel(offsets, aliased, *refs):
    count = len(offsets)
    pieces = refs[aliased : aliased + count]
    out_ref = refs[aliased + count]
    held, in_sems, out_sem = refs[aliased + count + 1 :]
    total = held.shape[0]
    step = math.gcd(32, *(piece.shape[0] for piece in pieces))
    moves = []
    for piece, offset in zip(pieces, offsets):
        for first in range(0, piece.shape[0], step):
            at = len(moves) * step
            slot = held.at[pl.ds(at, step)]
            moves.append((
                pltpu.make_async_copy(piece.at[pl.ds(first, step)], slot, in_sems.at[len(moves)]),
                pltpu.make_async_copy(slot, out_ref.at[pl.ds(offset + first, step)], out_sem),
            ))
    for inward, _ in moves:
        inward.start()
    for inward, outward in moves:
        inward.wait()
        outward.start()
    pltpu.make_async_copy(held, out_ref.at[pl.ds(0, total)], out_sem).wait()


def place(result, shape, pieces, offsets):
    aliased = int(result is not None)
    operands = ([result] if aliased else []) + pieces
    total = sum(p.shape[0] for p in pieces)
    return pl.pallas_call(
        functools.partial(place_kernel, offsets, aliased),
        in_specs=[pl.BlockSpec(memory_space=pltpu.HBM)] * len(operands),
        out_specs=pl.BlockSpec(memory_space=pltpu.HBM),
        out_shape=jax.ShapeDtypeStruct(shape, jnp.bfloat16),
        scratch_shapes=[
            pltpu.VMEM((total,) + shape[1:], jnp.bfloat16),
            pltpu.SemaphoreType.DMA((total // math.gcd(32, *(p.shape[0] for p in pieces)),)),
            pltpu.SemaphoreType.DMA,
        ],
        input_output_aliases={0: 0} if aliased else {},
        compiler_params=PARAMS,
        cost_estimate=pl.CostEstimate(
            flops=0, bytes_accessed=4 * sum(p.size for p in pieces), transcendentals=0
        ),
    )(*operands)


def body(vectors, coupling_table, factor_index, level_order):
    devices = lax.axis_size("gx") * lax.axis_size("gy")
    middle_bits = lax.axis_size("gy").bit_length() - 1
    levels = coupling_table.shape[0]
    blocks, rhs, rank = vectors.shape
    units = blocks // devices
    far_units = units - units // 4
    spread = devices * far_units

    def exchange(array):
        return lax.all_to_all(array, AXES, split_axis=0, concat_axis=0, tiled=True)

    def partner(array, level):
        axis, bit = ("gy", level) if level < middle_bits else ("gx", level - middle_bits)
        return lax.ppermute(array, axis, [(i, i ^ 1 << bit) for i in range(lax.axis_size(axis))])

    def near_level(near, level, other=None, **more):
        other = partner(near, level) if other is None else other
        return apply_level(near, other, table, near_index, level_order, level, **more)

    arrived = exchange(pack(vectors, factor_index, devices, far_units))
    table = jnp.swapaxes(coupling_table, 2, 3)
    half = (blocks - spread) // 2
    last_middle = middle_bits - 1
    if units > far_units:
        near_index = factor_index[spread:].reshape(-1)
        near = near_level(vectors[spread:], 0)
        first, second = near[:half], near[half:]
        for level in range(1, last_middle):
            first = near_level(first, level)
        for level in range(1, last_middle - 1):
            second = near_level(second, level, offset=half)
        first_other = partner(first, last_middle)
        second_other = partner(second, last_middle - 1)
    index = arrived[:, far_units * rhs].astype(jnp.int32)
    far = apply_all_levels(arrived, far_units, rhs, table, index, level_order)
    if units == far_units:
        return exchange(far).reshape(vectors.shape)
    far, first_other, near_index = lax.optimization_barrier((far, first_other, near_index))
    second = near_level(second, last_middle - 1, second_other, offset=half)
    second_other = partner(second, last_middle)
    far = exchange(far).reshape(spread, rhs, rank)
    near = near_level(
        jnp.concatenate([first, second]),
        last_middle,
        jnp.concatenate([first_other, second_other]),
        weight=HEAVY,
    )
    for level in range(middle_bits, levels):
        near = near_level(near, level)
    result = place(None, vectors.shape, [near], [spread])
    return place(result, vectors.shape, [far], [0])


def solution(mesh):
    placed = (P(AXES, None, None), P(), P(AXES, None, None), P())
    return jax.shard_map(
        body, mesh=mesh, in_specs=placed, out_specs=P(AXES, None, None), check_vma=False
    )
```

```python
import functools
import math

import jax
import jax.numpy as jnp
from jax import lax
from jax.experimental import pallas as pl
from jax.experimental.pallas import tpu as pltpu
from jax.sharding import PartitionSpec as P

AXES = ("gx", "gy")
LOAD_FACTOR = 7
HEAVY = 50
PACK_PARAMS = pltpu.CompilerParams(vmem_limit_bytes=58 * 1024 * 1024)
PARAMS = pltpu.CompilerParams(vmem_limit_bytes=24 * 1024 * 1024)


def levels_kernel(some, order_ref, index_ref, field_ref, table_ref, out_ref, even, odd):
    devices, share, rhs, rank = out_ref.shape
    levels = order_ref.shape[0]
    for level in some:
        target = out_ref if level == some[-1] else (even, odd)[(level + 1) % 2]
        slot = order_ref[level]

        def load(d, j):
            if level == 0:
                return field_ref[d, pl.ds(rhs * j, rhs), :]
            if level == some[0]:
                return field_ref[d, j]
            return (even, odd)[level % 2][d, j]

        def entries(d, j):
            at = (j * levels + slot) * 2
            return table_ref[slot, index_ref[d, at]], table_ref[slot, index_ref[d, at + 1]]

        def one_pair(pair, carry):
            low = ((pair >> level) << (level + 1)) | (pair & ((1 << level) - 1))
            high = low + (1 << level)
            for j in range(share):
                both = jnp.concatenate([load(low, j), load(high, j)], axis=1)
                low_own, low_other = entries(low, j)
                high_own, high_other = entries(high, j)
                coupling = jnp.concatenate(
                    [jnp.concatenate([low_own, low_other], axis=0), jnp.concatenate([high_other, high_own], axis=0)],
                    axis=1,
                )
                product = jnp.dot(both, coupling, preferred_element_type=jnp.float32).astype(jnp.bfloat16)
                target[low, j] = product[:, :rank]
                target[high, j] = product[:, rank:]
            return carry

        lax.fori_loop(0, devices // 2, one_pair, 0, unroll=8)


def apply_levels(some, payload, share, rhs, table, index, order):
    devices, rank = payload.shape[0], payload.shape[-1]
    levels = len(some)
    shape = (devices, share, rhs, rank)
    blocks = devices * share
    return pl.pallas_call(
        functools.partial(levels_kernel, some),
        grid_spec=pltpu.PrefetchScalarGridSpec(
            num_scalar_prefetch=2,
            grid=(),
            in_specs=[pl.BlockSpec(memory_space=pltpu.VMEM)] * 2,
            out_specs=pl.BlockSpec(memory_space=pltpu.VMEM),
            scratch_shapes=[pltpu.VMEM(shape, jnp.bfloat16)] * 2,
        ),
        out_shape=jax.ShapeDtypeStruct(shape, jnp.bfloat16),
        compiler_params=PARAMS,
        cost_estimate=pl.CostEstimate(
            flops=levels * blocks * 4 * rhs * rank * rank,
            bytes_accessed=2 * (2 * blocks * rhs * rank + table.size),
            transcendentals=0,
        ),
    )(order, index, payload, table)


def pack_kernel(units, vectors_ref, index_ref, out_ref, held, in_sems, out_sems):
    devices, rows, rank = out_ref.shape
    rhs = vectors_ref.shape[1]
    levels, _, blocks = index_ref.shape
    used = units * rhs
    parts = in_sems.shape[0]
    size = devices // parts
    source = vectors_ref.at[pl.ds(0, devices * units)].reshape(devices, used, rank)
    inward = [
        pltpu.make_async_copy(
            source.at[pl.ds(p * size, size)], held.at[pl.ds(p * size, size), pl.ds(0, used)], in_sems.at[p]
        )
        for p in range(parts)
    ]
    for copy in inward:
        copy.start()

    def pick(shape, condition):
        first, second = (lax.broadcasted_iota(jnp.int32, shape, dim) for dim in (0, 1))
        return condition(first, second).astype(jnp.float32).astype(jnp.bfloat16)

    def product(left, right, contract):
        return lax.dot_general(left, right, ((contract[:1], contract[1:]), ((), ())), preferred_element_type=jnp.float32)

    width = -(-2 * levels // 16) * 16
    entries = jnp.zeros((width, blocks), jnp.float32)
    for slot in range(levels):
        spot = pick((width, 2), lambda r, t: r == 2 * slot + t)
        entries += product(spot, index_ref[slot].astype(jnp.float32).astype(jnp.bfloat16), (1, 0))
    entries = entries.astype(jnp.bfloat16)
    lanes = jnp.zeros((devices, rank), jnp.float32)
    for unit in range(units):
        chosen = product(pick((devices, blocks), lambda d, b: b == d * units + unit), entries, (1, 1))
        spot = pick((width, rank), lambda r, lane: (lane == unit * 2 * levels + r) & (r < 2 * levels))
        lanes += product(chosen.astype(jnp.bfloat16), spot, (1, 0))
    for d in range(devices):
        held[d, pl.ds(used, rows - used)] = jnp.broadcast_to(lanes[d : d + 1], (rows - used, rank)).astype(jnp.bfloat16)

    outward = [
        pltpu.make_async_copy(held.at[pl.ds(p * size, size)], out_ref.at[pl.ds(p * size, size)], out_sems.at[p])
        for p in range(parts)
    ]
    for arrival, departure in zip(inward, outward):
        arrival.wait()
        departure.start()
    for copy in outward:
        copy.wait()


def pack(vectors, factor_index, devices, units):
    blocks, rhs, rank = vectors.shape
    levels = factor_index.shape[1]
    assert units * levels * 2 <= rank
    shape = (devices, units * rhs + 8, rank)
    parts = 8
    return pl.pallas_call(
        functools.partial(pack_kernel, units),
        in_specs=[pl.BlockSpec(memory_space=pltpu.HBM), pl.BlockSpec(memory_space=pltpu.VMEM)],
        out_specs=pl.BlockSpec(memory_space=pltpu.HBM),
        out_shape=jax.ShapeDtypeStruct(shape, jnp.bfloat16),
        scratch_shapes=[pltpu.VMEM(shape, jnp.bfloat16)] + [pltpu.SemaphoreType.DMA((parts,))] * 2,
        compiler_params=PACK_PARAMS,
        cost_estimate=pl.CostEstimate(flops=0, bytes_accessed=4 * vectors.size, transcendentals=0),
    )(vectors, jnp.transpose(factor_index, (1, 2, 0)))


def one_level_kernel(level, offset, order_ref, index_ref, own_ref, other_ref, table_ref, out_ref):
    levels = order_ref.shape[0]
    slot = order_ref[level]

    def one_block(b, carry):
        at = ((offset + b) * levels + slot) * 2
        both = jnp.concatenate([own_ref[b], other_ref[b]], axis=1)
        coupling = jnp.concatenate([table_ref[slot, index_ref[at]], table_ref[slot, index_ref[at + 1]]], axis=0)
        out_ref[b] = jnp.dot(both, coupling, preferred_element_type=jnp.float32).astype(jnp.bfloat16)
        return carry

    lax.fori_loop(0, own_ref.shape[0], one_block, 0, unroll=16)


def apply_level(own, other, table, index, order, level, offset=0, weight=1):
    blocks, rhs, rank = own.shape
    return pl.pallas_call(
        functools.partial(one_level_kernel, level, offset),
        grid_spec=pltpu.PrefetchScalarGridSpec(
            num_scalar_prefetch=2,
            grid=(),
            in_specs=[pl.BlockSpec(memory_space=pltpu.VMEM)] * 3,
            out_specs=pl.BlockSpec(memory_space=pltpu.VMEM),
        ),
        out_shape=jax.ShapeDtypeStruct(own.shape, jnp.bfloat16),
        compiler_params=PARAMS,
        cost_estimate=pl.CostEstimate(
            flops=weight * LOAD_FACTOR * blocks * 4 * rhs * rank * rank,
            bytes_accessed=2 * (3 * own.size + table.size),
            transcendentals=0,
        ),
    )(order, index, own, other, table)


def place_kernel(offsets, aliased, *refs):
    count = len(offsets)
    pieces = refs[aliased : aliased + count]
    out_ref = refs[aliased + count]
    held, in_sems, out_sem = refs[aliased + count + 1 :]
    total = held.shape[0]
    step = math.gcd(32, *(piece.shape[0] for piece in pieces))
    moves = []
    for piece, offset in zip(pieces, offsets):
        for first in range(0, piece.shape[0], step):
            at = len(moves) * step
            slot = held.at[pl.ds(at, step)]
            moves.append((
                pltpu.make_async_copy(piece.at[pl.ds(first, step)], slot, in_sems.at[len(moves)]),
                pltpu.make_async_copy(slot, out_ref.at[pl.ds(offset + first, step)], out_sem),
            ))
    for inward, _ in moves:
        inward.start()
    for inward, outward in moves:
        inward.wait()
        outward.start()
    pltpu.make_async_copy(held, out_ref.at[pl.ds(0, total)], out_sem).wait()


def place(result, shape, pieces, offsets):
    aliased = int(result is not None)
    operands = ([result] if aliased else []) + pieces
    total = sum(p.shape[0] for p in pieces)
    return pl.pallas_call(
        functools.partial(place_kernel, offsets, aliased),
        in_specs=[pl.BlockSpec(memory_space=pltpu.HBM)] * len(operands),
        out_specs=pl.BlockSpec(memory_space=pltpu.HBM),
        out_shape=jax.ShapeDtypeStruct(shape, jnp.bfloat16),
        scratch_shapes=[
            pltpu.VMEM((total,) + shape[1:], jnp.bfloat16),
            pltpu.SemaphoreType.DMA((total // math.gcd(32, *(p.shape[0] for p in pieces)),)),
            pltpu.SemaphoreType.DMA,
        ],
        input_output_aliases={0: 0} if aliased else {},
        compiler_params=PARAMS,
        cost_estimate=pl.CostEstimate(
            flops=0, bytes_accessed=4 * sum(p.size for p in pieces), transcendentals=0
        ),
    )(*operands)


def body(vectors, coupling_table, factor_index, level_order):
    devices = lax.axis_size("gx") * lax.axis_size("gy")
    middle_bits = lax.axis_size("gy").bit_length() - 1
    levels = coupling_table.shape[0]
    blocks, rhs, rank = vectors.shape
    units = blocks // devices
    far_units = units - units // 4
    spread = devices * far_units

    def exchange(array):
        return lax.all_to_all(array, AXES, split_axis=0, concat_axis=0, tiled=True)

    def partner(array, level):
        axis, bit = ("gy", level) if level < middle_bits else ("gx", level - middle_bits)
        return lax.ppermute(array, axis, [(i, i ^ 1 << bit) for i in range(lax.axis_size(axis))])

    def near_level(near, level, other=None, **more):
        other = partner(near, level) if other is None else other
        return apply_level(near, other, table, near_index, level_order, level, **more)

    arrived = exchange(pack(vectors, factor_index, devices, far_units))
    table = jnp.swapaxes(coupling_table, 2, 3)
    half = (blocks - spread) // 2
    last_middle = middle_bits - 1
    if units > far_units:
        near_index = factor_index[spread:].reshape(-1)
        near = near_level(vectors[spread:], 0)
        first, second = near[:half], near[half:]
        for level in range(1, last_middle):
            first = near_level(first, level)
        for level in range(1, last_middle - 1):
            second = near_level(second, level, offset=half)
        first_other = partner(first, last_middle)
        second_other = partner(second, last_middle - 1)
    index = arrived[:, far_units * rhs].astype(jnp.int32)
    if units == far_units:
        far = apply_levels(range(levels), arrived, far_units, rhs, table, index, level_order)
        return exchange(far).reshape(vectors.shape)
    far = apply_levels(range(2), arrived, far_units, rhs, table, index, level_order)
    far, near_index = lax.optimization_barrier((far, near_index))
    second = near_level(second, last_middle - 1, second_other, offset=half)
    far, second = lax.optimization_barrier((far, second))
    second_other = partner(second, last_middle)
    far = apply_levels(range(2, levels), far, far_units, rhs, table, index, level_order)
    far, first_other = lax.optimization_barrier((far, first_other))
    far = exchange(far).reshape(spread, rhs, rank)
    near = near_level(
        jnp.concatenate([first, second]),
        last_middle,
        jnp.concatenate([first_other, second_other]),
        weight=HEAVY,
    )
    for level in range(middle_bits, levels):
        near = near_level(near, level)
    result = place(None, vectors.shape, [near], [spread])
    return place(result, vectors.shape, [far], [0])


def solution(mesh):
    placed = (P(AXES, None, None), P(), P(AXES, None, None), P())
    return jax.shard_map(
        body, mesh=mesh, in_specs=placed, out_specs=P(AXES, None, None), check_vma=False
    )
```

```python
import functools
import math

import jax
import jax.numpy as jnp
from jax import lax
from jax.experimental import pallas as pl
from jax.experimental.pallas import tpu as pltpu
from jax.sharding import PartitionSpec as P

AXES = ("gx", "gy")
LOAD_FACTOR = 7
HEAVY = 50
PACK_PARAMS = pltpu.CompilerParams(vmem_limit_bytes=58 * 1024 * 1024)
PARAMS = pltpu.CompilerParams(vmem_limit_bytes=24 * 1024 * 1024)


def levels_kernel(some, sends, order_ref, index_ref, field_ref, table_ref, out_ref, even, odd, sem):
    devices, share, rhs, rank = out_ref.shape
    levels = order_ref.shape[0]
    for level in some:
        last = level == some[-1]
        target = out_ref if last and not sends else (even, odd)[(level + 1) % 2]
        slot = order_ref[level]

        def load(d, j):
            if level == 0:
                return field_ref[d, pl.ds(rhs * j, rhs), :]
            if level == some[0]:
                return field_ref[d, j]
            return (even, odd)[level % 2][d, j]

        def entries(d, j):
            at = (j * levels + slot) * 2
            return table_ref[slot, index_ref[d, at]], table_ref[slot, index_ref[d, at + 1]]

        def one_pair(pair, carry):
            low = ((pair >> level) << (level + 1)) | (pair & ((1 << level) - 1))
            high = low + (1 << level)
            for j in range(share):
                both = jnp.concatenate([load(low, j), load(high, j)], axis=1)
                low_own, low_other = entries(low, j)
                high_own, high_other = entries(high, j)
                coupling = jnp.concatenate(
                    [jnp.concatenate([low_own, low_other], axis=0), jnp.concatenate([high_other, high_own], axis=0)],
                    axis=1,
                )
                product = jnp.dot(both, coupling, preferred_element_type=jnp.float32).astype(jnp.bfloat16)
                target[low, j] = product[:, :rank]
                target[high, j] = product[:, rank:]
            return carry

        if not (last and sends):
            lax.fori_loop(0, devices // 2, one_pair, 0, unroll=8)
            continue
        pairs = devices // 2
        for first in (0, pairs // 2):
            lax.fori_loop(first, first + pairs // 2, one_pair, 0, unroll=8)
            for begin in (first, pairs + first):
                done = pl.ds(begin, pairs // 2)
                pltpu.make_async_copy(target.at[done], out_ref.at[done], sem).start()
        pltpu.make_async_copy(target, out_ref, sem).wait()


def apply_levels(some, sends, payload, share, rhs, table, index, order):
    devices, rank = payload.shape[0], payload.shape[-1]
    levels = len(some)
    shape = (devices, share, rhs, rank)
    blocks = devices * share
    return pl.pallas_call(
        functools.partial(levels_kernel, some, sends),
        grid_spec=pltpu.PrefetchScalarGridSpec(
            num_scalar_prefetch=2,
            grid=(),
            in_specs=[pl.BlockSpec(memory_space=pltpu.VMEM)] * 2,
            out_specs=pl.BlockSpec(memory_space=pltpu.HBM if sends else pltpu.VMEM),
            scratch_shapes=[pltpu.VMEM(shape, jnp.bfloat16)] * 2 + [pltpu.SemaphoreType.DMA],
        ),
        out_shape=jax.ShapeDtypeStruct(shape, jnp.bfloat16),
        compiler_params=PARAMS,
        cost_estimate=pl.CostEstimate(
            flops=levels * blocks * 4 * rhs * rank * rank,
            bytes_accessed=2 * (2 * blocks * rhs * rank + table.size),
            transcendentals=0,
        ),
    )(order, index, payload, table)


def pack_kernel(units, vectors_ref, index_ref, out_ref, held, in_sems, out_sems):
    devices, rows, rank = out_ref.shape
    rhs = vectors_ref.shape[1]
    levels, _, blocks = index_ref.shape
    used = units * rhs
    parts = in_sems.shape[0]
    size = devices // parts
    source = vectors_ref.at[pl.ds(0, devices * units)].reshape(devices, used, rank)
    inward = [
        pltpu.make_async_copy(
            source.at[pl.ds(p * size, size)], held.at[pl.ds(p * size, size), pl.ds(0, used)], in_sems.at[p]
        )
        for p in range(parts)
    ]
    for copy in inward:
        copy.start()

    def pick(shape, condition):
        first, second = (lax.broadcasted_iota(jnp.int32, shape, dim) for dim in (0, 1))
        return condition(first, second).astype(jnp.float32).astype(jnp.bfloat16)

    def product(left, right, contract):
        return lax.dot_general(left, right, ((contract[:1], contract[1:]), ((), ())), preferred_element_type=jnp.float32)

    width = -(-2 * levels // 16) * 16
    entries = jnp.zeros((width, blocks), jnp.float32)
    for slot in range(levels):
        spot = pick((width, 2), lambda r, t: r == 2 * slot + t)
        entries += product(spot, index_ref[slot].astype(jnp.float32).astype(jnp.bfloat16), (1, 0))
    entries = entries.astype(jnp.bfloat16)
    lanes = jnp.zeros((devices, rank), jnp.float32)
    for unit in range(units):
        chosen = product(pick((devices, blocks), lambda d, b: b == d * units + unit), entries, (1, 1))
        spot = pick((width, rank), lambda r, lane: (lane == unit * 2 * levels + r) & (r < 2 * levels))
        lanes += product(chosen.astype(jnp.bfloat16), spot, (1, 0))
    for d in range(devices):
        held[d, pl.ds(used, rows - used)] = jnp.broadcast_to(lanes[d : d + 1], (rows - used, rank)).astype(jnp.bfloat16)

    outward = [
        pltpu.make_async_copy(held.at[pl.ds(p * size, size)], out_ref.at[pl.ds(p * size, size)], out_sems.at[p])
        for p in range(parts)
    ]
    for arrival, departure in zip(inward, outward):
        arrival.wait()
        departure.start()
    for copy in outward:
        copy.wait()


def pack(vectors, factor_index, devices, units):
    blocks, rhs, rank = vectors.shape
    levels = factor_index.shape[1]
    assert units * levels * 2 <= rank
    shape = (devices, units * rhs + 8, rank)
    parts = 8
    return pl.pallas_call(
        functools.partial(pack_kernel, units),
        in_specs=[pl.BlockSpec(memory_space=pltpu.HBM), pl.BlockSpec(memory_space=pltpu.VMEM)],
        out_specs=pl.BlockSpec(memory_space=pltpu.HBM),
        out_shape=jax.ShapeDtypeStruct(shape, jnp.bfloat16),
        scratch_shapes=[pltpu.VMEM(shape, jnp.bfloat16)] + [pltpu.SemaphoreType.DMA((parts,))] * 2,
        compiler_params=PACK_PARAMS,
        cost_estimate=pl.CostEstimate(flops=0, bytes_accessed=4 * vectors.size, transcendentals=0),
    )(vectors, jnp.transpose(factor_index, (1, 2, 0)))


def one_level_kernel(level, offset, order_ref, index_ref, own_ref, other_ref, table_ref, out_ref, *fetched):
    if fetched:
        held, sem = fetched
        copy = pltpu.make_async_copy(other_ref, held, sem)
        copy.start()
        copy.wait()
        other_ref = held
    levels = order_ref.shape[0]
    slot = order_ref[level]

    def one_block(b, carry):
        at = ((offset + b) * levels + slot) * 2
        both = jnp.concatenate([own_ref[b], other_ref[b]], axis=1)
        coupling = jnp.concatenate([table_ref[slot, index_ref[at]], table_ref[slot, index_ref[at + 1]]], axis=0)
        out_ref[b] = jnp.dot(both, coupling, preferred_element_type=jnp.float32).astype(jnp.bfloat16)
        return carry

    lax.fori_loop(0, own_ref.shape[0], one_block, 0, unroll=16)


def apply_level(own, other, table, index, order, level, offset=0, weight=1, fetch=False):
    blocks, rhs, rank = own.shape
    return pl.pallas_call(
        functools.partial(one_level_kernel, level, offset),
        grid_spec=pltpu.PrefetchScalarGridSpec(
            num_scalar_prefetch=2,
            grid=(),
            in_specs=[
                pl.BlockSpec(memory_space=pltpu.VMEM),
                pl.BlockSpec(memory_space=pltpu.HBM if fetch else pltpu.VMEM),
                pl.BlockSpec(memory_space=pltpu.VMEM),
            ],
            out_specs=pl.BlockSpec(memory_space=pltpu.VMEM),
            scratch_shapes=[pltpu.VMEM(own.shape, own.dtype), pltpu.SemaphoreType.DMA] if fetch else [],
        ),
        out_shape=jax.ShapeDtypeStruct(own.shape, jnp.bfloat16),
        compiler_params=PARAMS,
        cost_estimate=pl.CostEstimate(
            flops=weight * LOAD_FACTOR * blocks * 4 * rhs * rank * rank,
            bytes_accessed=2 * (3 * own.size + table.size),
            transcendentals=0,
        ),
    )(order, index, own, other, table)


def place_kernel(offsets, aliased, *refs):
    count = len(offsets)
    pieces = refs[aliased : aliased + count]
    out_ref = refs[aliased + count]
    held, in_sems, out_sem = refs[aliased + count + 1 :]
    total = held.shape[0]
    step = math.gcd(32, *(piece.shape[0] for piece in pieces))
    moves = []
    for piece, offset in zip(pieces, offsets):
        for first in range(0, piece.shape[0], step):
            at = len(moves) * step
            slot = held.at[pl.ds(at, step)]
            moves.append((
                pltpu.make_async_copy(piece.at[pl.ds(first, step)], slot, in_sems.at[len(moves)]),
                pltpu.make_async_copy(slot, out_ref.at[pl.ds(offset + first, step)], out_sem),
            ))
    for inward, _ in moves:
        inward.start()
    for inward, outward in moves:
        inward.wait()
        outward.start()
    pltpu.make_async_copy(held, out_ref.at[pl.ds(0, total)], out_sem).wait()


def place(result, shape, pieces, offsets):
    aliased = int(result is not None)
    operands = ([result] if aliased else []) + pieces
    total = sum(p.shape[0] for p in pieces)
    return pl.pallas_call(
        functools.partial(place_kernel, offsets, aliased),
        in_specs=[pl.BlockSpec(memory_space=pltpu.HBM)] * len(operands),
        out_specs=pl.BlockSpec(memory_space=pltpu.HBM),
        out_shape=jax.ShapeDtypeStruct(shape, jnp.bfloat16),
        scratch_shapes=[
            pltpu.VMEM((total,) + shape[1:], jnp.bfloat16),
            pltpu.SemaphoreType.DMA((total // math.gcd(32, *(p.shape[0] for p in pieces)),)),
            pltpu.SemaphoreType.DMA,
        ],
        input_output_aliases={0: 0} if aliased else {},
        compiler_params=PARAMS,
        cost_estimate=pl.CostEstimate(
            flops=0, bytes_accessed=4 * sum(p.size for p in pieces), transcendentals=0
        ),
    )(*operands)


def body(vectors, coupling_table, factor_index, level_order):
    devices = lax.axis_size("gx") * lax.axis_size("gy")
    middle_bits = lax.axis_size("gy").bit_length() - 1
    levels = coupling_table.shape[0]
    blocks, rhs, rank = vectors.shape
    units = blocks // devices
    far_units = units - units // 4
    spread = devices * far_units

    def exchange(array):
        return lax.all_to_all(array, AXES, split_axis=0, concat_axis=0, tiled=True)

    def partner(array, level):
        axis, bit = ("gy", level) if level < middle_bits else ("gx", level - middle_bits)
        return lax.ppermute(array, axis, [(i, i ^ 1 << bit) for i in range(lax.axis_size(axis))])

    def near_level(near, level, other=None, **more):
        other = partner(near, level) if other is None else other
        return apply_level(near, other, table, near_index, level_order, level, **more)

    arrived = exchange(pack(vectors, factor_index, devices, far_units))
    table = jnp.swapaxes(coupling_table, 2, 3)
    half = (blocks - spread) // 2
    last_middle = middle_bits - 1
    if units > far_units:
        near_index = factor_index[spread:].reshape(-1)
        near = near_level(vectors[spread:], 0)
        first, second = near[:half], near[half:]
        for level in range(1, last_middle):
            first = near_level(first, level)
        for level in range(1, last_middle - 1):
            second = near_level(second, level, offset=half)
        first_other = partner(first, last_middle)
        second_other = partner(second, last_middle - 1)
    index = arrived[:, far_units * rhs].astype(jnp.int32)
    if units == far_units:
        far = apply_levels(range(levels), False, arrived, far_units, rhs, table, index, level_order)
        return exchange(far).reshape(vectors.shape)
    far = apply_levels(range(2), False, arrived, far_units, rhs, table, index, level_order)
    far, near_index = lax.optimization_barrier((far, near_index))
    second = near_level(second, last_middle - 1, second_other, offset=half, fetch=True)
    far, second = lax.optimization_barrier((far, second))
    second_other = partner(second, last_middle)
    far = apply_levels(range(2, levels), True, far, far_units, rhs, table, index, level_order)
    far, first_other = lax.optimization_barrier((far, first_other))
    far = exchange(far).reshape(spread, rhs, rank)
    near = near_level(
        jnp.concatenate([first, second]),
        last_middle,
        jnp.concatenate([first_other, second_other]),
        weight=HEAVY,
    )
    for level in range(middle_bits, levels):
        near = near_level(near, level)
    result = place(None, vectors.shape, [near], [spread])
    return place(result, vectors.shape, [far], [0])


def solution(mesh):
    placed = (P(AXES, None, None), P(), P(AXES, None, None), P())
    return jax.shard_map(
        body, mesh=mesh, in_specs=placed, out_specs=P(AXES, None, None), check_vma=False
    )
```

```python
import functools
import math

import jax
import jax.numpy as jnp
from jax import lax
from jax.experimental import pallas as pl
from jax.experimental.pallas import tpu as pltpu
from jax.sharding import PartitionSpec as P

AXES = ("gx", "gy")
LOAD_FACTOR = 7
HEAVY = 50
PACK_PARAMS = pltpu.CompilerParams(vmem_limit_bytes=58 * 1024 * 1024)
PARAMS = pltpu.CompilerParams(vmem_limit_bytes=24 * 1024 * 1024)


def levels_kernel(some, order_ref, index_ref, field_ref, table_ref, out_ref, even, odd):
    devices, share, rhs, rank = out_ref.shape
    levels = order_ref.shape[0]
    for level in some:
        target = out_ref if level == some[-1] else (even, odd)[(level + 1) % 2]
        slot = order_ref[level]

        def load(d, j):
            if level == 0:
                return field_ref[d, pl.ds(rhs * j, rhs), :]
            if level == some[0]:
                return field_ref[d, j]
            return (even, odd)[level % 2][d, j]

        def entries(d, j):
            at = (j * levels + slot) * 2
            return table_ref[slot, index_ref[d, at]], table_ref[slot, index_ref[d, at + 1]]

        def one_pair(pair, carry):
            low = ((pair >> level) << (level + 1)) | (pair & ((1 << level) - 1))
            high = low + (1 << level)
            for j in range(share):
                both = jnp.concatenate([load(low, j), load(high, j)], axis=1)
                low_own, low_other = entries(low, j)
                high_own, high_other = entries(high, j)
                coupling = jnp.concatenate(
                    [jnp.concatenate([low_own, low_other], axis=0), jnp.concatenate([high_other, high_own], axis=0)],
                    axis=1,
                )
                product = jnp.dot(both, coupling, preferred_element_type=jnp.float32).astype(jnp.bfloat16)
                target[low, j] = product[:, :rank]
                target[high, j] = product[:, rank:]
            return carry

        lax.fori_loop(0, devices // 2, one_pair, 0, unroll=8)


def apply_levels(some, payload, share, rhs, table, index, order):
    devices, rank = payload.shape[0], payload.shape[-1]
    levels = len(some)
    shape = (devices, share, rhs, rank)
    blocks = devices * share
    return pl.pallas_call(
        functools.partial(levels_kernel, some),
        grid_spec=pltpu.PrefetchScalarGridSpec(
            num_scalar_prefetch=2,
            grid=(),
            in_specs=[pl.BlockSpec(memory_space=pltpu.VMEM)] * 2,
            out_specs=pl.BlockSpec(memory_space=pltpu.VMEM),
            scratch_shapes=[pltpu.VMEM(shape, jnp.bfloat16)] * 2,
        ),
        out_shape=jax.ShapeDtypeStruct(shape, jnp.bfloat16),
        compiler_params=PARAMS,
        cost_estimate=pl.CostEstimate(
            flops=levels * blocks * 4 * rhs * rank * rank,
            bytes_accessed=2 * (2 * blocks * rhs * rank + table.size),
            transcendentals=0,
        ),
    )(order, index, payload, table)


def pack_kernel(units, vectors_ref, far_index_ref, out_ref, held, index_ref, index_sem, in_sems, out_sems):
    devices, rows, rank = out_ref.shape
    rhs = vectors_ref.shape[1]
    levels, _, blocks = index_ref.shape
    used = units * rhs
    parts = in_sems.shape[0]
    size = devices // parts
    source = vectors_ref.at[pl.ds(0, devices * units)].reshape(devices, used, rank)
    inward = [
        pltpu.make_async_copy(
            source.at[pl.ds(p * size, size)], held.at[pl.ds(p * size, size), pl.ds(0, used)], in_sems.at[p]
        )
        for p in range(parts)
    ]
    for copy in inward:
        copy.start()
    fetch = pltpu.make_async_copy(far_index_ref, index_ref, index_sem)
    fetch.start()
    fetch.wait()

    def pick(shape, condition):
        first, second = (lax.broadcasted_iota(jnp.int32, shape, dim) for dim in (0, 1))
        return condition(first, second).astype(jnp.float32).astype(jnp.bfloat16)

    def product(left, right, contract):
        return lax.dot_general(left, right, ((contract[:1], contract[1:]), ((), ())), preferred_element_type=jnp.float32)

    width = -(-2 * levels // 16) * 16
    entries = jnp.zeros((width, blocks), jnp.float32)
    for slot in range(levels):
        spot = pick((width, 2), lambda r, t: r == 2 * slot + t)
        entries += product(spot, index_ref[slot].astype(jnp.float32).astype(jnp.bfloat16), (1, 0))
    entries = entries.astype(jnp.bfloat16)
    lanes = jnp.zeros((devices, rank), jnp.float32)
    for unit in range(units):
        chosen = product(pick((devices, blocks), lambda d, b: b == d * units + unit), entries, (1, 1))
        spot = pick((width, rank), lambda r, lane: (lane == unit * 2 * levels + r) & (r < 2 * levels))
        lanes += product(chosen.astype(jnp.bfloat16), spot, (1, 0))
    for d in range(devices):
        held[d, pl.ds(used, rows - used)] = jnp.broadcast_to(lanes[d : d + 1], (rows - used, rank)).astype(jnp.bfloat16)

    outward = [
        pltpu.make_async_copy(held.at[pl.ds(p * size, size)], out_ref.at[pl.ds(p * size, size)], out_sems.at[p])
        for p in range(parts)
    ]
    for arrival, departure in zip(inward, outward):
        arrival.wait()
        departure.start()
    for copy in outward:
        copy.wait()


def pack(vectors, factor_index, devices, units):
    blocks, rhs, rank = vectors.shape
    levels = factor_index.shape[1]
    assert units * levels * 2 <= rank
    shape = (devices, units * rhs + 8, rank)
    parts = 8
    return pl.pallas_call(
        functools.partial(pack_kernel, units),
        in_specs=[pl.BlockSpec(memory_space=pltpu.HBM)] * 2,
        out_specs=pl.BlockSpec(memory_space=pltpu.HBM),
        out_shape=jax.ShapeDtypeStruct(shape, jnp.bfloat16),
        scratch_shapes=[pltpu.VMEM(shape, jnp.bfloat16), pltpu.VMEM((levels, 2, blocks), jnp.int32)]
        + [pltpu.SemaphoreType.DMA] + [pltpu.SemaphoreType.DMA((parts,))] * 2,
        compiler_params=PACK_PARAMS,
        cost_estimate=pl.CostEstimate(flops=0, bytes_accessed=4 * vectors.size, transcendentals=0),
    )(vectors, jnp.transpose(factor_index, (1, 2, 0)))


def one_level_kernel(level, offset, order_ref, index_ref, own_ref, other_ref, table_ref, out_ref):
    levels = order_ref.shape[0]
    slot = order_ref[level]

    def one_block(b, carry):
        at = ((offset + b) * levels + slot) * 2
        both = jnp.concatenate([own_ref[b], other_ref[b]], axis=1)
        coupling = jnp.concatenate([table_ref[slot, index_ref[at]], table_ref[slot, index_ref[at + 1]]], axis=0)
        out_ref[b] = jnp.dot(both, coupling, preferred_element_type=jnp.float32).astype(jnp.bfloat16)
        return carry

    lax.fori_loop(0, own_ref.shape[0], one_block, 0, unroll=16)


def apply_level(own, other, table, index, order, level, offset=0, weight=1):
    blocks, rhs, rank = own.shape
    return pl.pallas_call(
        functools.partial(one_level_kernel, level, offset),
        grid_spec=pltpu.PrefetchScalarGridSpec(
            num_scalar_prefetch=2,
            grid=(),
            in_specs=[pl.BlockSpec(memory_space=pltpu.VMEM)] * 3,
            out_specs=pl.BlockSpec(memory_space=pltpu.VMEM),
        ),
        out_shape=jax.ShapeDtypeStruct(own.shape, jnp.bfloat16),
        compiler_params=PARAMS,
        cost_estimate=pl.CostEstimate(
            flops=weight * LOAD_FACTOR * blocks * 4 * rhs * rank * rank,
            bytes_accessed=2 * (3 * own.size + table.size),
            transcendentals=0,
        ),
    )(order, index, own, other, table)


def place_kernel(offsets, aliased, *refs):
    count = len(offsets)
    pieces = refs[aliased : aliased + count]
    out_ref = refs[aliased + count]
    held, in_sems, out_sem = refs[aliased + count + 1 :]
    total = held.shape[0]
    step = math.gcd(16, *(piece.shape[0] for piece in pieces))
    moves = []
    for piece, offset in zip(pieces, offsets):
        for first in range(0, piece.shape[0], step):
            at = len(moves) * step
            slot = held.at[pl.ds(at, step)]
            moves.append((
                pltpu.make_async_copy(piece.at[pl.ds(first, step)], slot, in_sems.at[len(moves)]),
                pltpu.make_async_copy(slot, out_ref.at[pl.ds(offset + first, step)], out_sem),
            ))
    for inward, _ in moves:
        inward.start()
    for inward, outward in moves:
        inward.wait()
        outward.start()
    pltpu.make_async_copy(held, out_ref.at[pl.ds(0, total)], out_sem).wait()


def place(result, shape, pieces, offsets):
    aliased = int(result is not None)
    operands = ([result] if aliased else []) + pieces
    total = sum(p.shape[0] for p in pieces)
    return pl.pallas_call(
        functools.partial(place_kernel, offsets, aliased),
        in_specs=[pl.BlockSpec(memory_space=pltpu.HBM)] * len(operands),
        out_specs=pl.BlockSpec(memory_space=pltpu.HBM),
        out_shape=jax.ShapeDtypeStruct(shape, jnp.bfloat16),
        scratch_shapes=[
            pltpu.VMEM((total,) + shape[1:], jnp.bfloat16),
            pltpu.SemaphoreType.DMA((total // math.gcd(16, *(p.shape[0] for p in pieces)),)),
            pltpu.SemaphoreType.DMA,
        ],
        input_output_aliases={0: 0} if aliased else {},
        compiler_params=PARAMS,
        cost_estimate=pl.CostEstimate(
            flops=0, bytes_accessed=4 * sum(p.size for p in pieces), transcendentals=0
        ),
    )(*operands)


def body(vectors, coupling_table, factor_index, level_order):
    devices = lax.axis_size("gx") * lax.axis_size("gy")
    middle_bits = lax.axis_size("gy").bit_length() - 1
    levels = coupling_table.shape[0]
    blocks, rhs, rank = vectors.shape
    units = blocks // devices
    far_units = units - units // 4
    spread = devices * far_units

    def exchange(array):
        return lax.all_to_all(array, AXES, split_axis=0, concat_axis=0, tiled=True)

    def partner(array, level):
        axis, bit = ("gy", level) if level < middle_bits else ("gx", level - middle_bits)
        return lax.ppermute(array, axis, [(i, i ^ 1 << bit) for i in range(lax.axis_size(axis))])

    def near_level(near, level, other=None, **more):
        other = partner(near, level) if other is None else other
        return apply_level(near, other, table, near_index, level_order, level, **more)

    arrived = exchange(pack(vectors, factor_index, devices, far_units))
    table = jnp.swapaxes(coupling_table, 2, 3)
    half = (blocks - spread) // 2
    last_middle = middle_bits - 1
    if units > far_units:
        near_index = factor_index[spread:].reshape(-1)
        near = near_level(vectors[spread:], 0)
        first, second = near[:half], near[half:]
        for level in range(1, last_middle):
            first = near_level(first, level)
        for level in range(1, last_middle - 1):
            second = near_level(second, level, offset=half)
        first_other = partner(first, last_middle)
        second_other = partner(second, last_middle - 1)
    index = arrived[:, far_units * rhs].astype(jnp.int32)
    if units == far_units:
        far = apply_levels(range(levels), arrived, far_units, rhs, table, index, level_order)
        return exchange(far).reshape(vectors.shape)
    far = apply_levels(range(2), arrived, far_units, rhs, table, index, level_order)
    far, near_index = lax.optimization_barrier((far, near_index))
    second = near_level(second, last_middle - 1, second_other, offset=half)
    far, second = lax.optimization_barrier((far, second))
    second_other = partner(second, last_middle)
    far = apply_levels(range(2, levels), far, far_units, rhs, table, index, level_order)
    far, first_other = lax.optimization_barrier((far, first_other))
    far = exchange(far).reshape(spread, rhs, rank)
    near = near_level(
        jnp.concatenate([first, second]),
        last_middle,
        jnp.concatenate([first_other, second_other]),
        weight=HEAVY,
    )
    for level in range(middle_bits, levels):
        near = near_level(near, level)
    result = place(None, vectors.shape, [near], [spread])
    return place(result, vectors.shape, [far], [0])


def solution(mesh):
    placed = (P(AXES, None, None), P(), P(AXES, None, None), P())
    return jax.shard_map(
        body, mesh=mesh, in_specs=placed, out_specs=P(AXES, None, None), check_vma=False
    )
```

```python
import functools
import math

import jax
import jax.numpy as jnp
from jax import lax
from jax.experimental import pallas as pl
from jax.experimental.pallas import tpu as pltpu
from jax.sharding import PartitionSpec as P

AXES = ("gx", "gy")
LOAD_FACTOR = 7
HEAVY = 50
PACK_PARAMS = pltpu.CompilerParams(vmem_limit_bytes=58 * 1024 * 1024)
PARAMS = pltpu.CompilerParams(vmem_limit_bytes=24 * 1024 * 1024)


def levels_kernel(some, order_ref, index_ref, field_ref, table_ref, out_ref, even, odd):
    devices, share, rhs, rank = out_ref.shape
    levels = order_ref.shape[0]
    for level in some:
        target = out_ref if level == some[-1] else (even, odd)[(level + 1) % 2]
        slot = order_ref[level]

        def load(d, j):
            if level == 0:
                return field_ref[d, pl.ds(rhs * j, rhs), :]
            if level == some[0]:
                return field_ref[d, j]
            return (even, odd)[level % 2][d, j]

        def entries(d, j):
            at = (j * levels + slot) * 2
            return table_ref[slot, index_ref[d, at]], table_ref[slot, index_ref[d, at + 1]]

        def one_pair(pair, carry):
            low = ((pair >> level) << (level + 1)) | (pair & ((1 << level) - 1))
            high = low + (1 << level)
            for j in range(share):
                both = jnp.concatenate([load(low, j), load(high, j)], axis=1)
                low_own, low_other = entries(low, j)
                high_own, high_other = entries(high, j)
                coupling = jnp.concatenate(
                    [jnp.concatenate([low_own, low_other], axis=0), jnp.concatenate([high_other, high_own], axis=0)],
                    axis=1,
                )
                product = jnp.dot(both, coupling, preferred_element_type=jnp.float32).astype(jnp.bfloat16)
                target[low, j] = product[:, :rank]
                target[high, j] = product[:, rank:]
            return carry

        lax.fori_loop(0, devices // 2, one_pair, 0, unroll=8)


def apply_levels(some, payload, share, rhs, table, index, order):
    devices, rank = payload.shape[0], payload.shape[-1]
    levels = len(some)
    shape = (devices, share, rhs, rank)
    blocks = devices * share
    return pl.pallas_call(
        functools.partial(levels_kernel, some),
        grid_spec=pltpu.PrefetchScalarGridSpec(
            num_scalar_prefetch=2,
            grid=(),
            in_specs=[pl.BlockSpec(memory_space=pltpu.VMEM)] * 2,
            out_specs=pl.BlockSpec(memory_space=pltpu.VMEM),
            scratch_shapes=[pltpu.VMEM(shape, jnp.bfloat16)] * 2,
        ),
        out_shape=jax.ShapeDtypeStruct(shape, jnp.bfloat16),
        compiler_params=PARAMS,
        cost_estimate=pl.CostEstimate(
            flops=levels * blocks * 4 * rhs * rank * rank,
            bytes_accessed=2 * (2 * blocks * rhs * rank + table.size),
            transcendentals=0,
        ),
    )(order, index, payload, table)


def pack_kernel(units, vectors_ref, index_ref, out_ref, held, in_sems, out_sems):
    devices, rows, rank = out_ref.shape
    rhs = vectors_ref.shape[1]
    levels, _, blocks = index_ref.shape
    used = units * rhs
    parts = in_sems.shape[0]
    size = devices // parts
    source = vectors_ref.at[pl.ds(0, devices * units)].reshape(devices, used, rank)
    inward = [
        pltpu.make_async_copy(
            source.at[pl.ds(p * size, size)], held.at[pl.ds(p * size, size), pl.ds(0, used)], in_sems.at[p]
        )
        for p in range(parts)
    ]
    for copy in inward:
        copy.start()

    def pick(shape, condition):
        first, second = (lax.broadcasted_iota(jnp.int32, shape, dim) for dim in (0, 1))
        return condition(first, second).astype(jnp.float32).astype(jnp.bfloat16)

    def product(left, right, contract):
        return lax.dot_general(left, right, ((contract[:1], contract[1:]), ((), ())), preferred_element_type=jnp.float32)

    width = -(-2 * levels // 16) * 16
    entries = jnp.zeros((width, blocks), jnp.float32)
    for slot in range(levels):
        spot = pick((width, 2), lambda r, t: r == 2 * slot + t)
        entries += product(spot, index_ref[slot].astype(jnp.float32).astype(jnp.bfloat16), (1, 0))
    entries = entries.astype(jnp.bfloat16)
    lanes = jnp.zeros((devices, rank), jnp.float32)
    for unit in range(units):
        chosen = product(pick((devices, blocks), lambda d, b: b == d * units + unit), entries, (1, 1))
        spot = pick((width, rank), lambda r, lane: (lane == unit * 2 * levels + r) & (r < 2 * levels))
        lanes += product(chosen.astype(jnp.bfloat16), spot, (1, 0))
    for d in range(devices):
        held[d, pl.ds(used, rows - used)] = jnp.broadcast_to(lanes[d : d + 1], (rows - used, rank)).astype(jnp.bfloat16)

    outward = [
        pltpu.make_async_copy(held.at[pl.ds(p * size, size)], out_ref.at[pl.ds(p * size, size)], out_sems.at[p])
        for p in range(parts)
    ]
    for arrival, departure in zip(inward, outward):
        arrival.wait()
        departure.start()
    for copy in outward:
        copy.wait()


def pack(vectors, factor_index, devices, units):
    blocks, rhs, rank = vectors.shape
    levels = factor_index.shape[1]
    assert units * levels * 2 <= rank
    shape = (devices, units * rhs + 8, rank)
    parts = 8
    return pl.pallas_call(
        functools.partial(pack_kernel, units),
        in_specs=[pl.BlockSpec(memory_space=pltpu.HBM), pl.BlockSpec(memory_space=pltpu.VMEM)],
        out_specs=pl.BlockSpec(memory_space=pltpu.HBM),
        out_shape=jax.ShapeDtypeStruct(shape, jnp.bfloat16),
        scratch_shapes=[pltpu.VMEM(shape, jnp.bfloat16)] + [pltpu.SemaphoreType.DMA((parts,))] * 2,
        compiler_params=PACK_PARAMS,
        cost_estimate=pl.CostEstimate(flops=0, bytes_accessed=4 * vectors.size, transcendentals=0),
    )(vectors, jnp.transpose(factor_index, (1, 2, 0)))


def one_level_kernel(level, offset, order_ref, index_ref, own_ref, other_ref, table_ref, out_ref):
    levels = order_ref.shape[0]
    slot = order_ref[level]

    def one_block(b, carry):
        at = ((offset + b) * levels + slot) * 2
        both = jnp.concatenate([own_ref[b], other_ref[b]], axis=1)
        coupling = jnp.concatenate([table_ref[slot, index_ref[at]], table_ref[slot, index_ref[at + 1]]], axis=0)
        out_ref[b] = jnp.dot(both, coupling, preferred_element_type=jnp.float32).astype(jnp.bfloat16)
        return carry

    lax.fori_loop(0, own_ref.shape[0], one_block, 0, unroll=16)


def apply_level(own, other, table, index, order, level, offset=0, weight=1):
    blocks, rhs, rank = own.shape
    return pl.pallas_call(
        functools.partial(one_level_kernel, level, offset),
        grid_spec=pltpu.PrefetchScalarGridSpec(
            num_scalar_prefetch=2,
            grid=(),
            in_specs=[pl.BlockSpec(memory_space=pltpu.VMEM)] * 3,
            out_specs=pl.BlockSpec(memory_space=pltpu.VMEM),
        ),
        out_shape=jax.ShapeDtypeStruct(own.shape, jnp.bfloat16),
        compiler_params=PARAMS,
        cost_estimate=pl.CostEstimate(
            flops=weight * LOAD_FACTOR * blocks * 4 * rhs * rank * rank,
            bytes_accessed=2 * (3 * own.size + table.size),
            transcendentals=0,
        ),
    )(order, index, own, other, table)


def place_kernel(offsets, aliased, *refs):
    count = len(offsets)
    pieces = refs[aliased : aliased + count]
    out_ref = refs[aliased + count]
    held, in_sems, out_sem = refs[aliased + count + 1 :]
    total = held.shape[0]
    step = math.gcd(32, *(piece.shape[0] for piece in pieces))
    moves = []
    for piece, offset in zip(pieces, offsets):
        for first in range(0, piece.shape[0], step):
            at = len(moves) * step
            slot = held.at[pl.ds(at, step)]
            moves.append((
                pltpu.make_async_copy(piece.at[pl.ds(first, step)], slot, in_sems.at[len(moves)]),
                pltpu.make_async_copy(slot, out_ref.at[pl.ds(offset + first, step)], out_sem),
            ))
    for inward, _ in moves:
        inward.start()
    for inward, outward in moves:
        inward.wait()
        outward.start()
    pltpu.make_async_copy(held, out_ref.at[pl.ds(0, total)], out_sem).wait()


def place(result, shape, pieces, offsets):
    aliased = int(result is not None)
    operands = ([result] if aliased else []) + pieces
    total = sum(p.shape[0] for p in pieces)
    return pl.pallas_call(
        functools.partial(place_kernel, offsets, aliased),
        in_specs=[pl.BlockSpec(memory_space=pltpu.HBM)] * len(operands),
        out_specs=pl.BlockSpec(memory_space=pltpu.HBM),
        out_shape=jax.ShapeDtypeStruct(shape, jnp.bfloat16),
        scratch_shapes=[
            pltpu.VMEM((total,) + shape[1:], jnp.bfloat16),
            pltpu.SemaphoreType.DMA((total // math.gcd(32, *(p.shape[0] for p in pieces)),)),
            pltpu.SemaphoreType.DMA,
        ],
        input_output_aliases={0: 0} if aliased else {},
        compiler_params=PARAMS,
        cost_estimate=pl.CostEstimate(
            flops=0, bytes_accessed=4 * sum(p.size for p in pieces), transcendentals=0
        ),
    )(*operands)


def body(vectors, coupling_table, factor_index, level_order):
    devices = lax.axis_size("gx") * lax.axis_size("gy")
    middle_bits = lax.axis_size("gy").bit_length() - 1
    levels = coupling_table.shape[0]
    blocks, rhs, rank = vectors.shape
    units = blocks // devices
    far_units = units - units // 4
    spread = devices * far_units

    def exchange(array):
        return lax.all_to_all(array, AXES, split_axis=0, concat_axis=0, tiled=True)

    def partner(array, level):
        axis, bit = ("gy", level) if level < middle_bits else ("gx", level - middle_bits)
        return lax.ppermute(array, axis, [(i, i ^ 1 << bit) for i in range(lax.axis_size(axis))])

    def near_level(near, level, other=None, **more):
        other = partner(near, level) if other is None else other
        return apply_level(near, other, table, near_index, level_order, level, **more)

    arrived = exchange(pack(vectors, factor_index, devices, far_units))
    table = jnp.swapaxes(coupling_table, 2, 3)
    half = (blocks - spread) // 2
    last_middle = middle_bits - 1
    if units > far_units:
        near_index = factor_index[spread:].reshape(-1)
        near = near_level(vectors[spread:], 0)
        first, second = near[:half], near[half:]
        for level in range(1, last_middle):
            first = near_level(first, level)
        for level in range(1, last_middle - 1):
            second = near_level(second, level, offset=half)
        first_other = partner(first, last_middle)
        second_other = partner(second, last_middle - 1)
    if units > far_units:
        second = near_level(second, last_middle - 1, second_other, offset=half)
        arrived, second = lax.optimization_barrier((arrived, second))
        second_other = partner(second, last_middle)
    index = arrived[:, far_units * rhs].astype(jnp.int32)
    far = apply_levels(range(levels), arrived, far_units, rhs, table, index, level_order)
    if units == far_units:
        return exchange(far).reshape(vectors.shape)
    far, first_other = lax.optimization_barrier((far, first_other))
    far = exchange(far).reshape(spread, rhs, rank)
    near = near_level(
        jnp.concatenate([first, second]),
        last_middle,
        jnp.concatenate([first_other, second_other]),
        weight=HEAVY,
    )
    for level in range(middle_bits, levels):
        near = near_level(near, level)
    result = place(None, vectors.shape, [near], [spread])
    return place(result, vectors.shape, [far], [0])


def solution(mesh):
    placed = (P(AXES, None, None), P(), P(AXES, None, None), P())
    return jax.shard_map(
        body, mesh=mesh, in_specs=placed, out_specs=P(AXES, None, None), check_vma=False
    )
```

```python
import functools
import math

import jax
import jax.numpy as jnp
from jax import lax
from jax.experimental import pallas as pl
from jax.experimental.pallas import tpu as pltpu
from jax.sharding import PartitionSpec as P

AXES = ("gx", "gy")
LOAD_FACTOR = 7
HEAVY = 50
PACK_PARAMS = pltpu.CompilerParams(vmem_limit_bytes=58 * 1024 * 1024)
PARAMS = pltpu.CompilerParams(vmem_limit_bytes=24 * 1024 * 1024)


def levels_kernel(some, order_ref, index_ref, field_ref, table_ref, out_ref, even, odd):
    devices, share, rhs, rank = out_ref.shape
    levels = order_ref.shape[0]
    for level in some:
        target = out_ref if level == some[-1] else (even, odd)[(level + 1) % 2]
        slot = order_ref[level]

        def load(d, j):
            if level == 0:
                return field_ref[d, pl.ds(rhs * j, rhs), :]
            if level == some[0]:
                return field_ref[d, j]
            return (even, odd)[level % 2][d, j]

        def entries(d, j):
            at = (j * levels + slot) * 2
            return table_ref[slot, index_ref[d, at]], table_ref[slot, index_ref[d, at + 1]]

        def one_pair(pair, carry):
            low = ((pair >> level) << (level + 1)) | (pair & ((1 << level) - 1))
            high = low + (1 << level)
            for j in range(share):
                both = jnp.concatenate([load(low, j), load(high, j)], axis=1)
                low_own, low_other = entries(low, j)
                high_own, high_other = entries(high, j)
                coupling = jnp.concatenate(
                    [jnp.concatenate([low_own, low_other], axis=0), jnp.concatenate([high_other, high_own], axis=0)],
                    axis=1,
                )
                product = jnp.dot(both, coupling, preferred_element_type=jnp.float32).astype(jnp.bfloat16)
                target[low, j] = product[:, :rank]
                target[high, j] = product[:, rank:]
            return carry

        lax.fori_loop(0, devices // 2, one_pair, 0, unroll=8)


def apply_levels(some, payload, share, rhs, table, index, order):
    devices, rank = payload.shape[0], payload.shape[-1]
    levels = len(some)
    shape = (devices, share, rhs, rank)
    blocks = devices * share
    return pl.pallas_call(
        functools.partial(levels_kernel, some),
        grid_spec=pltpu.PrefetchScalarGridSpec(
            num_scalar_prefetch=2,
            grid=(),
            in_specs=[pl.BlockSpec(memory_space=pltpu.VMEM)] * 2,
            out_specs=pl.BlockSpec(memory_space=pltpu.VMEM),
            scratch_shapes=[pltpu.VMEM(shape, jnp.bfloat16)] * 2,
        ),
        out_shape=jax.ShapeDtypeStruct(shape, jnp.bfloat16),
        compiler_params=PARAMS,
        cost_estimate=pl.CostEstimate(
            flops=levels * blocks * 4 * rhs * rank * rank,
            bytes_accessed=2 * (2 * blocks * rhs * rank + table.size),
            transcendentals=0,
        ),
    )(order, index, payload, table)


def pack_kernel(units, vectors_ref, index_ref, out_ref, held, in_sems, out_sems):
    devices, rows, rank = out_ref.shape
    rhs = vectors_ref.shape[1]
    levels, _, blocks = index_ref.shape
    used = units * rhs
    parts = in_sems.shape[0]
    size = devices // parts
    source = vectors_ref.at[pl.ds(0, devices * units)].reshape(devices, used, rank)
    inward = [
        pltpu.make_async_copy(
            source.at[pl.ds(p * size, size)], held.at[pl.ds(p * size, size), pl.ds(0, used)], in_sems.at[p]
        )
        for p in range(parts)
    ]
    for copy in inward:
        copy.start()

    def pick(shape, condition):
        first, second = (lax.broadcasted_iota(jnp.int32, shape, dim) for dim in (0, 1))
        return condition(first, second).astype(jnp.float32).astype(jnp.bfloat16)

    def product(left, right, contract):
        return lax.dot_general(left, right, ((contract[:1], contract[1:]), ((), ())), preferred_element_type=jnp.float32)

    width = -(-2 * levels // 16) * 16
    entries = jnp.zeros((width, blocks), jnp.float32)
    for slot in range(levels):
        spot = pick((width, 2), lambda r, t: r == 2 * slot + t)
        entries += product(spot, index_ref[slot].astype(jnp.float32).astype(jnp.bfloat16), (1, 0))
    entries = entries.astype(jnp.bfloat16)
    lanes = jnp.zeros((devices, rank), jnp.float32)
    for unit in range(units):
        chosen = product(pick((devices, blocks), lambda d, b: b == d * units + unit), entries, (1, 1))
        spot = pick((width, rank), lambda r, lane: (lane == unit * 2 * levels + r) & (r < 2 * levels))
        lanes += product(chosen.astype(jnp.bfloat16), spot, (1, 0))
    for d in range(devices):
        held[d, pl.ds(used, rows - used)] = jnp.broadcast_to(lanes[d : d + 1], (rows - used, rank)).astype(jnp.bfloat16)

    outward = [
        pltpu.make_async_copy(held.at[pl.ds(p * size, size)], out_ref.at[pl.ds(p * size, size)], out_sems.at[p])
        for p in range(parts)
    ]
    for arrival, departure in zip(inward, outward):
        arrival.wait()
        departure.start()
    for copy in outward:
        copy.wait()


def pack(vectors, factor_index, devices, units):
    blocks, rhs, rank = vectors.shape
    levels = factor_index.shape[1]
    assert units * levels * 2 <= rank
    shape = (devices, units * rhs + 8, rank)
    parts = 8
    return pl.pallas_call(
        functools.partial(pack_kernel, units),
        in_specs=[pl.BlockSpec(memory_space=pltpu.HBM), pl.BlockSpec(memory_space=pltpu.VMEM)],
        out_specs=pl.BlockSpec(memory_space=pltpu.HBM),
        out_shape=jax.ShapeDtypeStruct(shape, jnp.bfloat16),
        scratch_shapes=[pltpu.VMEM(shape, jnp.bfloat16)] + [pltpu.SemaphoreType.DMA((parts,))] * 2,
        compiler_params=PACK_PARAMS,
        cost_estimate=pl.CostEstimate(flops=0, bytes_accessed=4 * vectors.size, transcendentals=0),
    )(vectors, jnp.transpose(factor_index, (1, 2, 0)))


def one_level_kernel(level, offset, given, order_ref, index_ref, own_ref, other_ref, table_ref, out_ref):
    levels = order_ref.shape[0]
    slot = order_ref[level]

    def one_block(b, carry):
        at = ((offset + b) * levels + slot) * 2
        both = jnp.concatenate([own_ref[b], other_ref[b]], axis=1)
        pair = [table_ref[slot, index_ref[at]], table_ref[slot, index_ref[at + 1]]]
        coupling = jnp.concatenate(pair, axis=1 if given else 0)
        out_ref[b] = lax.dot_general(
            both, coupling, (((1,), (1 if given else 0,)), ((), ())), preferred_element_type=jnp.float32
        ).astype(jnp.bfloat16)
        return carry

    lax.fori_loop(0, own_ref.shape[0], one_block, 0, unroll=16)


def apply_level(own, other, table, index, order, level, offset=0, weight=1, given=False):
    blocks, rhs, rank = own.shape
    return pl.pallas_call(
        functools.partial(one_level_kernel, level, offset, given),
        grid_spec=pltpu.PrefetchScalarGridSpec(
            num_scalar_prefetch=2,
            grid=(),
            in_specs=[pl.BlockSpec(memory_space=pltpu.VMEM)] * 3,
            out_specs=pl.BlockSpec(memory_space=pltpu.VMEM),
        ),
        out_shape=jax.ShapeDtypeStruct(own.shape, jnp.bfloat16),
        compiler_params=PARAMS,
        cost_estimate=pl.CostEstimate(
            flops=weight * LOAD_FACTOR * blocks * 4 * rhs * rank * rank,
            bytes_accessed=2 * (3 * own.size + table.size),
            transcendentals=0,
        ),
    )(order, index, own, other, table)


def place_kernel(offsets, aliased, *refs):
    count = len(offsets)
    pieces = refs[aliased : aliased + count]
    out_ref = refs[aliased + count]
    held, in_sems, out_sem = refs[aliased + count + 1 :]
    total = held.shape[0]
    step = math.gcd(32, *(piece.shape[0] for piece in pieces))
    moves = []
    for piece, offset in zip(pieces, offsets):
        for first in range(0, piece.shape[0], step):
            at = len(moves) * step
            slot = held.at[pl.ds(at, step)]
            moves.append((
                pltpu.make_async_copy(piece.at[pl.ds(first, step)], slot, in_sems.at[len(moves)]),
                pltpu.make_async_copy(slot, out_ref.at[pl.ds(offset + first, step)], out_sem),
            ))
    for inward, _ in moves:
        inward.start()
    for inward, outward in moves:
        inward.wait()
        outward.start()
    pltpu.make_async_copy(held, out_ref.at[pl.ds(0, total)], out_sem).wait()


def place(result, shape, pieces, offsets):
    aliased = int(result is not None)
    operands = ([result] if aliased else []) + pieces
    total = sum(p.shape[0] for p in pieces)
    return pl.pallas_call(
        functools.partial(place_kernel, offsets, aliased),
        in_specs=[pl.BlockSpec(memory_space=pltpu.HBM)] * len(operands),
        out_specs=pl.BlockSpec(memory_space=pltpu.HBM),
        out_shape=jax.ShapeDtypeStruct(shape, jnp.bfloat16),
        scratch_shapes=[
            pltpu.VMEM((total,) + shape[1:], jnp.bfloat16),
            pltpu.SemaphoreType.DMA((total // math.gcd(32, *(p.shape[0] for p in pieces)),)),
            pltpu.SemaphoreType.DMA,
        ],
        input_output_aliases={0: 0} if aliased else {},
        compiler_params=PARAMS,
        cost_estimate=pl.CostEstimate(
            flops=0, bytes_accessed=4 * sum(p.size for p in pieces), transcendentals=0
        ),
    )(*operands)


def body(vectors, coupling_table, factor_index, level_order):
    devices = lax.axis_size("gx") * lax.axis_size("gy")
    middle_bits = lax.axis_size("gy").bit_length() - 1
    levels = coupling_table.shape[0]
    blocks, rhs, rank = vectors.shape
    units = blocks // devices
    far_units = units - units // 4
    spread = devices * far_units

    def exchange(array):
        return lax.all_to_all(array, AXES, split_axis=0, concat_axis=0, tiled=True)

    def partner(array, level):
        axis, bit = ("gy", level) if level < middle_bits else ("gx", level - middle_bits)
        return lax.ppermute(array, axis, [(i, i ^ 1 << bit) for i in range(lax.axis_size(axis))])

    def near_level(near, level, other=None, **more):
        other = partner(near, level) if other is None else other
        return apply_level(near, other, table, near_index, level_order, level, **more)

    arrived = exchange(pack(vectors, factor_index, devices, far_units))
    table = jnp.swapaxes(coupling_table, 2, 3)
    half = (blocks - spread) // 2
    last_middle = middle_bits - 1
    if units > far_units:
        near_index = factor_index[spread:].reshape(-1)
        near = vectors[spread:]
        near = apply_level(near, partner(near, 0), coupling_table, near_index, level_order, 0, given=True)
        first, second = near[:half], near[half:]
        for level in range(1, last_middle):
            first = near_level(first, level)
        for level in range(1, last_middle - 1):
            second = near_level(second, level, offset=half)
        first_other = partner(first, last_middle)
        second_other = partner(second, last_middle - 1)
    index = arrived[:, far_units * rhs].astype(jnp.int32)
    if units == far_units:
        far = apply_levels(range(levels), arrived, far_units, rhs, table, index, level_order)
        return exchange(far).reshape(vectors.shape)
    far = apply_levels(range(2), arrived, far_units, rhs, table, index, level_order)
    far, near_index = lax.optimization_barrier((far, near_index))
    second = near_level(second, last_middle - 1, second_other, offset=half)
    far, second = lax.optimization_barrier((far, second))
    second_other = partner(second, last_middle)
    far = apply_levels(range(2, levels), far, far_units, rhs, table, index, level_order)
    far, first_other = lax.optimization_barrier((far, first_other))
    far = exchange(far).reshape(spread, rhs, rank)
    near = near_level(
        jnp.concatenate([first, second]),
        last_middle,
        jnp.concatenate([first_other, second_other]),
        weight=HEAVY,
    )
    for level in range(middle_bits, levels):
        near = near_level(near, level)
    result = place(None, vectors.shape, [near], [spread])
    return place(result, vectors.shape, [far], [0])


def solution(mesh):
    placed = (P(AXES, None, None), P(), P(AXES, None, None), P())
    return jax.shard_map(
        body, mesh=mesh, in_specs=placed, out_specs=P(AXES, None, None), check_vma=False
    )
```
